256 devices in a mesh: expert: 16 (over x, y_lo, core), tensor: 2 (over y_hi), replica: 8 (over z).
Axes of the slice: x: 4, y: 4 (y_hi: 2, y_lo: 2; y = y_hi * 2 + y_lo), z: 8, core: 2. Of those that a mesh axis runs over, the one named last changes fastest.
Arguments:
- tokens: bfloat16 [2048, 3072], P('expert', 'replica'), may hold values from -6 to 6
- cotangent: bfloat16 [2048, 3072], P('expert', 'replica'), may hold values from -4 to 4
- gate_values: float32 [2048, 4], P('expert'), may hold values from 0.05 to 1
- expert_ids: int32 [2048, 4], P('expert'), may hold values from 0 to 15, all different within a row; in each aligned block of 128 rows (0 to 127, 128 to 255, ...) at most 48 rows name the same one
- gate_weight: bfloat16 [16, 3072, 5376], P('expert', 'replica', 'tensor'), may hold values from -0.109375 to 0.109375
- up_weight: bfloat16 [16, 3072, 5376], P('expert', 'replica', 'tensor'), may hold values from -0.109375 to 0.109375
- down_weight: bfloat16 [16, 5376, 3072], P('expert', 'tensor', 'replica'), may hold values from -0.078125 to 0.078125
- block_ids: int32 [16, 2], P('expert'), may hold values from 0 to 23, as said below
- feedback: bfloat16 [16, 3072, 5376], P('expert', 'replica', 'tensor'), may hold values from -6 to 6
Outputs:
- token_grad: bfloat16 [2048, 3072], P(('expert', 'tensor'), 'replica')
- block_sums: float32 [16, 2, 128, 5376], P('expert', None, None, 'tensor')
- new_feedback: bfloat16 [16, 3072, 5376], P('expert', 'replica', 'tensor')
The draws below stay inside these ranges and needn't reach their ends.
Inputs may be any that keep to these rules, and one draw needn't show every extreme that they name: `expert_ids`: in the rows of one token group no expert is named more than 48 times, and each row names 4 different experts. `block_ids`: for each expert the 2 block numbers are different.
All inputs are finite; a program needn't handle non-finite values.
Results may differ from the reference program's by a relative error of at most 0.03.
Values may be sent and summed in bfloat16 or wider, within the bound.
No kernel may reach another device: no remote copies, remote signals or barrier semaphores. Data moves between devices by JAX's collectives and lax.ppermute only.
A program may use at most 128 MiB of HBM per device.

```python
import math
import jax
import jax.numpy as jnp
import numpy as np
from jax import lax

D = 3072
FF = 5376
TOP = 4
TOK_GRP = 128
BLOCK = 128
SELECT = 2
EXPERTS = 16
FF_DEV = 2688
CAP = 48
NBLK = 24
TOKENS = 2048
N_EXPERT = 16
N_TENSOR = 2
N_REPLICA = 8


def draw_block_ids(key, part):
    key = jax.random.fold_in(key, 7)
    keys = jax.random.split(key, EXPERTS)
    chosen = jax.vmap(lambda k: jax.random.permutation(k, NBLK - 2)[:SELECT] + 1)(keys).astype(jnp.int32)
    high_owner = jax.random.randint(jax.random.fold_in(key, 1001), (), 0, EXPERTS)
    low_owner = jax.random.randint(jax.random.fold_in(key, 1002), (), 0, EXPERTS)
    owners = jnp.arange(EXPERTS, dtype=jnp.int32)
    first = jnp.where(owners == high_owner, jnp.int32(NBLK - 1), chosen[:, 0])
    second = jnp.where(owners == low_owner, jnp.int32(0), chosen[:, 1])
    chosen = chosen.at[:, 0].set(first)
    chosen = chosen.at[:, 1].set(second)
    return chosen.astype(jnp.int32)


def steps_of(own_key, shape, shards, smallest, high):
    def one(axis_at, blocks):
        heights = jax.random.uniform(jax.random.fold_in(jax.random.fold_in(own_key, 6), axis_at), (blocks,), jnp.float32, smallest / len(shards), high / len(shards))
        return jnp.repeat(jnp.exp(heights), shape[axis_at] // blocks).reshape((-1,) + (1,) * (len(shape) - axis_at - 1))

    factor_of = one(*shards[0])
    for cut in shards[1:]:
        factor_of = factor_of * one(*cut)
    return factor_of


def deal_out(own_key, own, number, rows, number_of, top, limit, slope):
    order = jax.random.permutation(own_key, number_of)
    packed, common = portions_of(number_of, rows * top, limit, slope, True), portions_of(number_of, rows * top, limit, slope, False)
    places = jnp.arange(number_of)

    def named(tallies, turn):
        used = int((tallies > 0).sum())
        fixed = max(1, used // 4)
        shifted = fixed + (places - fixed + turn * (used - fixed)) % max(1, number_of - fixed)
        return jnp.zeros((number_of,), jnp.int32).at[order[jnp.where(places < fixed, places, shifted)]].set(jnp.asarray(tallies, jnp.int32))

    tallies = jnp.where(number % 4 == 0, named(packed, number // 4), named(common, number - number // 4 - 1))
    mixed = jax.random.permutation(jax.random.fold_in(own, 3), number_of)
    donor, sink = mixed[0:number_of // 2 * 2:2], mixed[1:number_of // 2 * 2:2]
    room = jnp.minimum(tallies[donor] - 1, limit - tallies[sink]) // 2
    room = jnp.where((donor == order[0]) | (sink == order[0]) | (tallies[sink] == 0), 0, jnp.maximum(room, 0))
    shifted = jax.random.randint(jax.random.fold_in(own, 4), (number_of // 2,), 0, 1 << 20) % (room + 1)
    tallies = tallies.at[donor].add(-shifted).at[sink].add(shifted)
    items = jnp.searchsorted(jnp.cumsum(tallies), jnp.arange(rows * top), side="right").astype(jnp.int32)
    listing = items.reshape(top, rows).T
    listing = listing[jax.random.permutation(jax.random.fold_in(own, 1), rows)]
    turn = jax.random.randint(jax.random.fold_in(own, 2), (rows, 1), 0, top)
    return jnp.take_along_axis(listing, (jnp.arange(top)[None, :] + turn) % top, axis=1)


def portions_of(number_of, total, bound, slope, full):
    loads = [(1 << 20) // math.isqrt(rank ** slope) + 1 for rank in range(1, number_of + 1)]
    largest = bound if full else min(bound, max(-(-total // number_of), total * loads[0] // sum(loads)))
    least = 1 if total - largest >= number_of - 1 else 0
    given, surplus = [largest] + [least] * (number_of - 1), total - largest - least * (number_of - 1)
    while surplus > 0:
        movable = [i for i in range(1, number_of) if given[i] < largest] or [i for i in range(1, number_of) if given[i] < bound]
        mass, left = sum([loads[i] for i in movable]), surplus
        for i in movable:
            more = min(bound - given[i], max(1, left * loads[i] // mass), surplus)
            given[i] = given[i] + more
            surplus = surplus - more
    return np.array(given)


def gaussian(own_key, dims, deviation, bound, shards=(), kind=jnp.bfloat16):
    entries = deviation * jax.random.normal(own_key, dims, jnp.float32)
    if shards:
        entries = entries * steps_of(own_key, dims, shards, -0.22, 0.18)
    return jnp.clip(entries, -bound, bound).astype(kind)


def setup_inputs(seed: int = 0) -> dict:
    splits = jax.random.split(jax.random.key(seed), 10)
    tokens = gaussian(splits[0], (TOKENS, D), 1.0, 6.0, ((0, 16), (1, 8)))
    cotangent = gaussian(splits[1], (TOKENS, D), 0.5, 4.0, ((0, 16), (1, 8)))
    gate_values = jnp.clip(jnp.exp(math.log(1.0) - 2.9957323 * jax.random.uniform(splits[2], (TOKENS, TOP), jnp.float32) ** steps_of(splits[2], (TOKENS, TOP), ((0, 16),), -0.2, 0.2)), 0.05, 1.0)
    expert_ids_keys = jax.random.split(jax.random.fold_in(splits[3], 1), TOKENS // TOK_GRP)
    expert_ids_turns = jax.random.permutation(jax.random.fold_in(splits[3], 3), TOKENS // TOK_GRP)
    expert_ids = jax.vmap(lambda own, number: deal_out(jax.random.fold_in(splits[3], 2), own, number, TOK_GRP, EXPERTS, TOP, CAP, 1))(expert_ids_keys, expert_ids_turns).reshape((TOKENS, TOP))
    gate_weight = gaussian(splits[4], (EXPERTS, D, FF), D ** -0.5, 0.109375, ((0, 16), (1, 8), (2, 2)))
    up_weight = gaussian(splits[5], (EXPERTS, D, FF), D ** -0.5, 0.109375, ((0, 16), (1, 8), (2, 2)))
    down_weight = gaussian(splits[6], (EXPERTS, FF, D), FF ** -0.5, 0.078125, ((0, 16), (1, 2), (2, 8)))
    block_ids = draw_block_ids(jax.random.fold_in(splits[9], 71), 0)
    feedback = gaussian(splits[8], (EXPERTS, D, FF), 1.0, 6.0, ((0, 16), (1, 8), (2, 2)))
    return {"tokens": tokens, "cotangent": cotangent, "gate_values": gate_values, "expert_ids": expert_ids, "gate_weight": gate_weight, "up_weight": up_weight, "down_weight": down_weight, "block_ids": block_ids, "feedback": feedback}


def routing_tables(expert_ids, gate_values, experts, capacity):
    tok_rows, top_count = expert_ids.shape
    flat_ids = expert_ids.reshape(-1)
    choose = (flat_ids[:, None] == jnp.arange(experts, dtype=jnp.int32)[None, :]).astype(jnp.int32)
    before = jnp.cumsum(choose, axis=0) - choose
    slot_index = jnp.sum(before * choose, axis=1).astype(jnp.int32)
    target = (flat_ids * capacity + slot_index).reshape(tok_rows, top_count)
    matches = target[None, :, :] == jnp.arange(experts * capacity, dtype=jnp.int32)[:, None, None]
    placing = jnp.any(matches, axis=2).astype(jnp.bfloat16)
    slot_gate = jnp.sum(jnp.where(matches, gate_values[None, :, :], jnp.float32(0.0)), axis=(1, 2))
    return placing, slot_gate


def replica_sum(operand, weight_shares, pattern):
    pieces = jnp.einsum(pattern, operand, weight_shares)
    pieces = lax.optimization_barrier(pieces.astype(jnp.bfloat16)).astype(jnp.float32)
    return jnp.sum(pieces, axis=0)


def one_expert(args):
    slot_rows, slot_grads, w_gate, w_up, w_down, stored, chosen = args
    slot_count = slot_rows.shape[0]
    share_width = D // N_REPLICA
    rows_float = slot_rows.astype(jnp.float32)
    row_shares = rows_float.reshape(slot_count, N_REPLICA, share_width)
    grad_shares = slot_grads.astype(jnp.float32).reshape(slot_count, N_REPLICA, share_width)
    gate_pre = replica_sum(row_shares, w_gate.astype(jnp.float32).reshape(N_REPLICA, share_width, FF), 'snd,ndf->nsf')
    up_pre = replica_sum(row_shares, w_up.astype(jnp.float32).reshape(N_REPLICA, share_width, FF), 'snd,ndf->nsf')
    hidden_grad = replica_sum(grad_shares, w_down.astype(jnp.float32).reshape(FF, N_REPLICA, share_width), 'snd,fnd->nsf')
    squashed = jax.nn.sigmoid(gate_pre)
    grad_gate = (hidden_grad * up_pre * squashed * (1.0 + gate_pre * (1.0 - squashed))).astype(jnp.bfloat16)
    grad_up = (hidden_grad * gate_pre * squashed).astype(jnp.bfloat16)
    split_gate = grad_gate.astype(jnp.float32).reshape(slot_count, N_TENSOR, FF_DEV)
    split_up = grad_up.astype(jnp.float32).reshape(slot_count, N_TENSOR, FF_DEV)
    shard_gate = w_gate.astype(jnp.float32).reshape(D, N_TENSOR, FF_DEV)
    shard_up = w_up.astype(jnp.float32).reshape(D, N_TENSOR, FF_DEV)
    parts = jnp.einsum('snf,dnf->nsd', split_gate, shard_gate) + jnp.einsum('snf,dnf->nsd', split_up, shard_up)
    parts = lax.optimization_barrier(parts.astype(jnp.bfloat16)).astype(jnp.float32)
    part_sum = jnp.sum(parts, axis=0)
    weight_grad = jnp.einsum('sd,sf->df', rows_float, grad_gate.astype(jnp.float32))
    gradient = weight_grad + stored.astype(jnp.float32)
    blocked = gradient.reshape(NBLK, BLOCK, FF)
    picked = jnp.take(blocked, chosen, axis=0)
    struck = jnp.any(chosen[:, None] == jnp.arange(NBLK, dtype=jnp.int32)[None, :], axis=0)
    retained = jnp.where(struck[:, None, None], jnp.float32(0.0), blocked).reshape(D, FF).astype(jnp.bfloat16)
    return part_sum, picked, retained


def reference(tokens, cotangent, gate_values, expert_ids, gate_weight, up_weight, down_weight, block_ids, feedback):
    token_groups = tokens.reshape(N_EXPERT, TOK_GRP, D).astype(jnp.float32)
    cotangent_groups = cotangent.reshape(N_EXPERT, TOK_GRP, D).astype(jnp.float32)
    route_groups = expert_ids.reshape(N_EXPERT, TOK_GRP, TOP)
    weight_groups = gate_values.reshape(N_EXPERT, TOK_GRP, TOP)
    placing, slot_gate = jax.vmap(lambda a, b: routing_tables(a, b, EXPERTS, CAP))(route_groups, weight_groups)
    place_float = placing.astype(jnp.float32)
    dispatched = jnp.einsum('sjt,std->sjd', place_float, token_groups).astype(jnp.bfloat16)
    dispatched_grads = (jnp.einsum('sjt,std->sjd', place_float, cotangent_groups) * slot_gate[:, :, None]).astype(jnp.bfloat16)
    dispatched = jnp.moveaxis(dispatched.reshape(N_EXPERT, EXPERTS, CAP, D), 1, 0).reshape(EXPERTS, N_EXPERT * CAP, D)
    dispatched_grads = jnp.moveaxis(dispatched_grads.reshape(N_EXPERT, EXPERTS, CAP, D), 1, 0).reshape(EXPERTS, N_EXPERT * CAP, D)
    part_sum, picked, retained = lax.map(one_expert, (dispatched, dispatched_grads, gate_weight, up_weight, down_weight, feedback, block_ids))
    returned = jnp.moveaxis(part_sum.reshape(EXPERTS, N_EXPERT, CAP, D), 1, 0).reshape(N_EXPERT, EXPERTS * CAP, D)
    gathered_grad = jnp.einsum('sjt,sjd->std', place_float, returned, precision=lax.Precision.HIGHEST)
    token_grad = gathered_grad.reshape(TOKENS, D).astype(jnp.bfloat16)
    return token_grad, picked, retained
```

```python
import jax
import jax.numpy as jnp
from jax import lax
from jax.experimental import pallas as pl
from jax.experimental.pallas import tpu as pltpu
from jax.sharding import PartitionSpec as P

BLOCK = 128


def routing_tables(expert_ids, gate_values, experts, capacity):
    tok_rows, top_count = expert_ids.shape
    flat_ids = expert_ids.reshape(-1)
    choose = (flat_ids[:, None] == jnp.arange(experts, dtype=jnp.int32)[None, :]).astype(jnp.int32)
    before = jnp.cumsum(choose, axis=0) - choose
    slot_index = jnp.sum(before * choose, axis=1)
    target = (flat_ids * capacity + slot_index).reshape(tok_rows, top_count)
    matches = target[None, :, :] == jnp.arange(experts * capacity, dtype=jnp.int32)[:, None, None]
    placing = jnp.any(matches, axis=2).astype(jnp.bfloat16)
    slot_gate = jnp.sum(jnp.where(matches, gate_values[None, :, :], jnp.float32(0.0)), axis=(1, 2))
    return (placing, slot_gate)


MIB = 1024 * 1024
SPARE = 48


def shift_by(distance, size):
    return [(i, (i + distance) % size) for i in range(size)]


def split_kernel(own_hidden, here_ref, gate_ref, up_ref, *refs):
    outs, turned = refs[:-1], refs[-1]
    columns = gate_ref.shape[1]

    @pl.loop(0, columns // BLOCK)
    def _(tile):
        at = pl.ds(pl.multiple_of(tile * BLOCK, BLOCK), BLOCK)
        turned[0, at, :] = gate_ref[:, at].T
        turned[1, at, :] = up_ref[:, at].T

    for d, out in enumerate(outs):
        owner = lax.rem(here_ref[0] + d, len(outs))
        rows = pl.ds(pl.multiple_of(owner * own_hidden, 16), own_hidden)
        out[:own_hidden, :] = turned[0, rows, :]
        out[own_hidden:, :] = turned[1, rows, :]


def split_weights(w_gate, w_up, here, shares):
    features, hidden = w_gate.shape
    own_hidden = hidden // shares
    piece = jax.ShapeDtypeStruct((2 * own_hidden, features), jnp.bfloat16)
    return pl.pallas_call(
        lambda *refs: split_kernel(own_hidden, *refs),
        in_specs=[
            pl.BlockSpec(memory_space=pltpu.SMEM),
            pl.BlockSpec(memory_space=pltpu.VMEM),
            pl.BlockSpec(memory_space=pltpu.VMEM),
        ],
        out_specs=[pl.BlockSpec(memory_space=pltpu.VMEM)] * shares,
        out_shape=[piece] * shares,
        scratch_shapes=[pltpu.VMEM((2, hidden, features), jnp.bfloat16)],
        cost_estimate=pl.CostEstimate(
            flops=0, bytes_accessed=8 * hidden * features, transcendentals=0
        ),
        compiler_params=pltpu.CompilerParams(vmem_limit_bytes=58 * MIB),
    )(here.reshape(1), w_gate, w_up)


def pick_kernel(at_ref, holds_ref, stored_ref, out_ref):
    wide, select = out_ref.shape[1], at_ref.shape[0]
    whole = stored_ref.shape[1] // wide
    rest = stored_ref.shape[1] - whole * wide
    for i in range(select):
        rows = stored_ref[pl.ds(pl.multiple_of(at_ref[i], BLOCK), BLOCK), :]
        rows = jnp.where(holds_ref[i] > 0, rows, jnp.zeros_like(rows))
        for c in range(whole):
            start = (c * select + i) * BLOCK
            out_ref[start : start + BLOCK, :] = rows[:, c * wide : (c + 1) * wide]
        out_ref[whole * select * BLOCK :, i * rest : (i + 1) * rest] = rows[:, whole * wide :]


def pick_stored(stored, held_at, holding, wide):
    high = held_at.shape[0] * BLOCK * stored.shape[1] // wide
    return pl.pallas_call(
        pick_kernel,
        in_specs=[
            pl.BlockSpec(memory_space=pltpu.SMEM),
            pl.BlockSpec(memory_space=pltpu.SMEM),
            pl.BlockSpec(memory_space=pltpu.VMEM),
        ],
        out_specs=pl.BlockSpec(memory_space=pltpu.VMEM),
        out_shape=jax.ShapeDtypeStruct((high, wide), jnp.bfloat16),
        cost_estimate=pl.CostEstimate(
            flops=0, bytes_accessed=2 * (stored.size + high * wide), transcendentals=0
        ),
        compiler_params=pltpu.CompilerParams(vmem_limit_bytes=24 * MIB),
    )(held_at, holding.astype(jnp.int32), stored)


def restore(packed, select, hidden):
    wide = packed.shape[1]
    whole = hidden // wide
    rest = hidden - whole * wide
    blocks = []
    for i in range(select):
        cuts = [packed[(c * select + i) * BLOCK :][:BLOCK] for c in range(whole)]
        cuts.append(packed[whole * select * BLOCK :, i * rest : (i + 1) * rest])
        blocks.append(jnp.concatenate(cuts, axis=1))
    return jnp.stack(blocks)


def hidden_kernel(weight_ref, rows_ref, extra_ref, out_ref):
    high = weight_ref.shape[0]
    out_ref[:high, :] = lax.dot_general(
        weight_ref[...],
        rows_ref[...],
        (((1,), (1,)), ((), ())),
        preferred_element_type=jnp.float32,
    ).astype(out_ref.dtype)
    out_ref[high:, :] = extra_ref[...]


def hidden_product(weight, rows, extra, steps):
    high, depth = weight.shape
    slots = rows.shape[0]
    total = high + extra.shape[0]
    return pl.pallas_call(
        hidden_kernel,
        grid=(steps,),
        in_specs=[
            pl.BlockSpec((high // steps, depth), lambda i: (i, 0)),
            pl.BlockSpec((slots, depth), lambda i: (0, 0)),
            pl.BlockSpec((extra.shape[0] // steps, slots), lambda i: (i, 0)),
        ],
        out_specs=pl.BlockSpec((total // steps, slots), lambda i: (i, 0)),
        out_shape=jax.ShapeDtypeStruct((total, slots), jnp.bfloat16),
        cost_estimate=pl.CostEstimate(
            flops=2 * high * depth * slots,
            bytes_accessed=2 * (high * depth + slots * depth + 2 * total * slots),
            transcendentals=0,
        ),
        compiler_params=pltpu.CompilerParams(vmem_limit_bytes=32 * MIB),
    )(weight, rows, extra)


def gates_kernel(rows_ref, grad_ref, *refs):
    weights, own_ref, shown_ref = refs[:-2], refs[-2], refs[-1]
    own_hidden, depth = own_ref.shape[0] // 2, weights[0].shape[1]
    pre = None
    for d, weight in enumerate(weights):
        term = lax.dot_general(
            weight[...],
            rows_ref[:, d * depth : (d + 1) * depth],
            (((1,), (1,)), ((), ())),
            preferred_element_type=jnp.float32,
        )
        pre = term if pre is None else pre + term
    gate_pre, up_pre = pre[:own_hidden], pre[own_hidden:]
    hidden_grad = grad_ref[:own_hidden, :].astype(jnp.float32)
    squashed = 1.0 / (1.0 + jnp.exp(-gate_pre))
    grad_gate = (hidden_grad * up_pre * squashed * (1.0 + gate_pre * (1.0 - squashed))).astype(
        own_ref.dtype
    )
    own_ref[:own_hidden, :] = grad_gate
    own_ref[own_hidden:, :] = (hidden_grad * gate_pre * squashed).astype(own_ref.dtype)
    shown_ref[:own_hidden, :] = grad_gate
    shown_ref[own_hidden:, :] = grad_ref[own_hidden:, :]


def hidden_gates(weights, rows, hidden_grad, tile):
    slots, width = rows.shape
    high, shown = weights[0].shape[0], hidden_grad.shape[0]
    whole = pl.BlockSpec(weights[0].shape, lambda i: (0, 0))
    return pl.pallas_call(
        gates_kernel,
        grid=(slots // tile,),
        in_specs=[
            pl.BlockSpec((tile, width), lambda i: (i, 0)),
            pl.BlockSpec((shown, tile), lambda i: (0, i)),
        ]
        + [whole] * len(weights),
        out_specs=[
            pl.BlockSpec((high, tile), lambda i: (0, i)),
            pl.BlockSpec((shown, tile), lambda i: (0, i)),
        ],
        out_shape=[
            jax.ShapeDtypeStruct((high, slots), jnp.bfloat16),
            jax.ShapeDtypeStruct((shown, slots), jnp.bfloat16),
        ],
        cost_estimate=pl.CostEstimate(
            flops=2 * high * width * slots,
            bytes_accessed=2 * (high * width + slots * width + (high + 2 * shown) * slots),
            transcendentals=high // 2 * slots,
        ),
        compiler_params=pltpu.CompilerParams(vmem_limit_bytes=56 * MIB),
    )(rows, hidden_grad, *weights)


def part_kernel(own_ref, *refs):
    weights, out_ref = refs[:-1], refs[-1]
    depth = weights[0].shape[1]
    own = own_ref[...].T
    for d, weight in enumerate(weights):
        out_ref[:, d * depth : (d + 1) * depth] = jnp.dot(
            own, weight[...], preferred_element_type=jnp.float32
        ).astype(out_ref.dtype)


def slot_parts(own, weights, tile):
    high, slots = own.shape
    width = weights[0].shape[1] * len(weights)
    whole = pl.BlockSpec(weights[0].shape, lambda i: (0, 0))
    return pl.pallas_call(
        part_kernel,
        grid=(slots // tile,),
        in_specs=[pl.BlockSpec((high, tile), lambda i: (0, i))] + [whole] * len(weights),
        out_specs=pl.BlockSpec((tile, width), lambda i: (i, 0)),
        out_shape=jax.ShapeDtypeStruct((slots, width), jnp.bfloat16),
        cost_estimate=pl.CostEstimate(
            flops=2 * high * width * slots,
            bytes_accessed=2 * (high * width + slots * width + high * slots),
            transcendentals=0,
        ),
        compiler_params=pltpu.CompilerParams(vmem_limit_bytes=56 * MIB),
    )(own, *weights)


def combine_kernel(behind_ref, placing_ref, parts_ref, out_ref):
    sides, shares, half, features = out_ref.shape
    for q in range(shares):
        at = pl.ds(pl.multiple_of(behind_ref[q] * features, BLOCK), features)
        rows = jnp.dot(
            placing_ref[...], parts_ref[:, at], preferred_element_type=jnp.float32
        ).astype(out_ref.dtype)
        for j in range(sides):
            out_ref[j, q] = rows[j * half : (j + 1) * half]


def combine(placing, parts, behind, sides):
    tok_rows, slots = placing.shape
    shares = behind.shape[0]
    features = parts.shape[1] // shares
    return pl.pallas_call(
        combine_kernel,
        in_specs=[
            pl.BlockSpec(memory_space=pltpu.SMEM),
            pl.BlockSpec(memory_space=pltpu.VMEM),
            pl.BlockSpec(memory_space=pltpu.VMEM),
        ],
        out_specs=pl.BlockSpec(memory_space=pltpu.VMEM),
        out_shape=jax.ShapeDtypeStruct(
            (sides, shares, tok_rows // sides, features), jnp.bfloat16
        ),
        cost_estimate=pl.CostEstimate(
            flops=2 * slots * tok_rows * features * shares,
            bytes_accessed=2 * (parts.size + placing.size + tok_rows * features * shares),
            transcendentals=0,
        ),
        compiler_params=pltpu.CompilerParams(vmem_limit_bytes=32 * MIB),
    )(behind, placing, parts)


def body(
    tokens,
    cotangent,
    gate_values,
    expert_ids,
    gate_weight,
    up_weight,
    down_weight,
    block_ids,
    feedback,
):
    groups = lax.axis_size("expert")
    shares = lax.axis_size("replica")
    sides = lax.axis_size("tensor")
    here = lax.axis_index("replica")
    experts = groups * gate_weight.shape[0]
    tok_rows, top_count = expert_ids.shape
    capacity = min(tok_rows, tok_rows * top_count * 3 // (2 * experts))
    features = tokens.shape[1]
    width = features * shares
    hidden = gate_weight.shape[2]
    own_hidden = hidden // shares
    stored = feedback[0]

    local_blocks = features // BLOCK
    local_ids = block_ids[0] - here * local_blocks
    holding = jnp.logical_and(local_ids >= 0, local_ids < local_blocks)
    held_at = jnp.clip(local_ids, 0, local_blocks - 1) * BLOCK
    select = local_ids.shape[0]

    pieces = split_weights(gate_weight[0], up_weight[0], here, shares)
    expert_ids, *pieces = lax.optimization_barrier((expert_ids, *pieces))

    def hand_out(d):
        return lax.ppermute(pieces[d], "replica", shift_by(d, shares))

    got = {d: hand_out(d) if d else pieces[0] for d in (0, 4, 3, 5, 2, 6, 1, 7)}

    padded = jnp.pad(tokens, ((0, SPARE), (0, 0)))
    gathered = lax.all_gather(padded, "replica", axis=0, tiled=False)

    placing, slot_gate = routing_tables(expert_ids, gate_values, experts, capacity)
    sent_grads = (
        jnp.dot(placing, cotangent, preferred_element_type=jnp.float32) * slot_gate[:, None]
    ).astype(jnp.bfloat16)
    sent_grads = sent_grads.reshape(experts, capacity, features)
    stored_rows = pick_stored(stored, held_at, holding, experts * capacity)
    sent_grads, stored_rows = lax.optimization_barrier((sent_grads, stored_rows))
    arrived_grads = lax.all_to_all(sent_grads, "expert", split_axis=0, concat_axis=0, tiled=True)
    grad_rows = arrived_grads.reshape(-1, features)
    hidden_part = hidden_product(down_weight[0], grad_rows, stored_rows, shares)
    hidden_part, got[4] = lax.optimization_barrier((hidden_part, got[4]))
    hidden_grad = lax.psum_scatter(hidden_part, "replica", scatter_dimension=0, tiled=True)

    behind = (here - jnp.arange(shares, dtype=jnp.int32)) % shares
    whole_tokens = jnp.take(gathered[:, :tok_rows], behind, axis=0)
    whole_tokens = whole_tokens.transpose(1, 0, 2).reshape(tok_rows, width)
    sent_rows = jnp.dot(placing, whole_tokens, preferred_element_type=jnp.float32)
    sent_rows = sent_rows.astype(jnp.bfloat16).reshape(experts, capacity, width)
    sent_rows, got[3], got[5] = lax.optimization_barrier((sent_rows, got[3], got[5]))
    arrived = lax.all_to_all(sent_rows, "expert", split_axis=0, concat_axis=0, tiled=True)
    slot_rows = arrived.reshape(-1, width)
    weights = [got[d] for d in range(shares)]

    own, shown = hidden_gates(weights, slot_rows, hidden_grad, 2 * BLOCK)
    partial_grad = slot_parts(own, weights, 2 * BLOCK).reshape(experts, capacity, width)
    returned = lax.all_to_all(partial_grad, "expert", split_axis=0, concat_axis=0, tiled=True)

    shown = lax.all_gather(shown, "replica", axis=0, tiled=False)
    grad_gate = shown[:, :own_hidden].reshape(hidden, -1)
    stored_rows = restore(
        shown[:, own_hidden:].reshape(-1, experts * capacity), select, hidden
    )

    gradient = jnp.einsum(
        "sd,fs->df", slot_rows[:, :features], grad_gate, preferred_element_type=jnp.float32
    ) + stored.astype(jnp.float32)
    struck = jnp.any(
        local_ids[:, None] == jnp.arange(local_blocks, dtype=jnp.int32)[None, :], axis=0
    )
    retained = (
        jnp.where(
            struck[:, None, None],
            jnp.float32(0.0),
            gradient.reshape(local_blocks, BLOCK, hidden),
        )
        .reshape(gradient.shape)
        .astype(jnp.bfloat16)
    )

    placed = (here - block_ids[0] // local_blocks) % shares
    picked_at = placed * features + block_ids[0] % local_blocks * BLOCK
    picked = jnp.concatenate(
        [
            lax.dynamic_slice_in_dim(slot_rows, picked_at[i], BLOCK, axis=1)
            for i in range(select)
        ],
        axis=1,
    )
    block_sums = jnp.einsum("sk,fs->kf", picked, grad_gate, preferred_element_type=jnp.float32)
    block_sums = block_sums.reshape(select, BLOCK, hidden) + stored_rows.astype(jnp.float32)
    combined = combine(placing.T, returned.reshape(experts * capacity, width), behind, sides)
    combined = combined.reshape(sides * shares, tok_rows // sides, features)
    collected = lax.all_to_all(
        combined, ("tensor", "replica"), split_axis=0, concat_axis=0, tiled=True
    )
    collected, retained, block_sums = lax.optimization_barrier((collected, retained, block_sums))
    token_grad = jnp.sum(collected.astype(jnp.float32), axis=0).astype(jnp.bfloat16)
    return (token_grad, block_sums[None], retained[None])


def solution(mesh):
    return jax.shard_map(
        body,
        mesh=mesh,
        in_specs=(
            P("expert", "replica"),
            P("expert", "replica"),
            P("expert", None),
            P("expert", None),
            P("expert", "replica", "tensor"),
            P("expert", "replica", "tensor"),
            P("expert", "tensor", "replica"),
            P("expert", None),
            P("expert", "replica", "tensor"),
        ),
        out_specs=(
            P(("expert", "tensor"), "replica"),
            P("expert", None, None, "tensor"),
            P("expert", "replica", "tensor"),
        ),
        check_vma=False,
    )
```

```python
import jax
import jax.numpy as jnp
from jax import lax
from jax.experimental import pallas as pl
from jax.experimental.pallas import tpu as pltpu
from jax.sharding import PartitionSpec as P

BLOCK = 128


def routing_tables(expert_ids, gate_values, experts, capacity):
    tok_rows, top_count = expert_ids.shape
    flat_ids = expert_ids.reshape(-1)
    choose = (flat_ids[:, None] == jnp.arange(experts, dtype=jnp.int32)[None, :]).astype(jnp.int32)
    before = jnp.cumsum(choose, axis=0) - choose
    slot_index = jnp.sum(before * choose, axis=1)
    target = (flat_ids * capacity + slot_index).reshape(tok_rows, top_count)
    matches = target[None, :, :] == jnp.arange(experts * capacity, dtype=jnp.int32)[:, None, None]
    placing = jnp.any(matches, axis=2).astype(jnp.bfloat16)
    slot_gate = jnp.sum(jnp.where(matches, gate_values[None, :, :], jnp.float32(0.0)), axis=(1, 2))
    return (placing, slot_gate)


MIB = 1024 * 1024
SPARE = 48


def shift_by(distance, size):
    return [(i, (i + distance) % size) for i in range(size)]


def split_kernel(own_hidden, here_ref, gate_ref, up_ref, *refs):
    outs, turned = refs[:-1], refs[-1]
    columns = gate_ref.shape[1]

    @pl.loop(0, columns // BLOCK)
    def _(tile):
        at = pl.ds(pl.multiple_of(tile * BLOCK, BLOCK), BLOCK)
        turned[0, at, :] = gate_ref[:, at].T
        turned[1, at, :] = up_ref[:, at].T

    for d, out in enumerate(outs):
        owner = lax.rem(here_ref[0] + d, len(outs))
        rows = pl.ds(pl.multiple_of(owner * own_hidden, 16), own_hidden)
        out[:own_hidden, :] = turned[0, rows, :]
        out[own_hidden:, :] = turned[1, rows, :]


def split_weights(w_gate, w_up, here, shares):
    features, hidden = w_gate.shape
    own_hidden = hidden // shares
    piece = jax.ShapeDtypeStruct((2 * own_hidden, features), jnp.bfloat16)
    return pl.pallas_call(
        lambda *refs: split_kernel(own_hidden, *refs),
        in_specs=[
            pl.BlockSpec(memory_space=pltpu.SMEM),
            pl.BlockSpec(memory_space=pltpu.VMEM),
            pl.BlockSpec(memory_space=pltpu.VMEM),
        ],
        out_specs=[pl.BlockSpec(memory_space=pltpu.VMEM)] * shares,
        out_shape=[piece] * shares,
        scratch_shapes=[pltpu.VMEM((2, hidden, features), jnp.bfloat16)],
        cost_estimate=pl.CostEstimate(
            flops=0, bytes_accessed=8 * hidden * features, transcendentals=0
        ),
        compiler_params=pltpu.CompilerParams(vmem_limit_bytes=58 * MIB),
    )(here.reshape(1), w_gate, w_up)


def pick_kernel(at_ref, holds_ref, stored_ref, out_ref):
    wide, select = out_ref.shape[1], at_ref.shape[0]
    whole = stored_ref.shape[1] // wide
    rest = stored_ref.shape[1] - whole * wide
    for i in range(select):
        rows = stored_ref[pl.ds(pl.multiple_of(at_ref[i], BLOCK), BLOCK), :]
        rows = jnp.where(holds_ref[i] > 0, rows, jnp.zeros_like(rows))
        for c in range(whole):
            start = (c * select + i) * BLOCK
            out_ref[start : start + BLOCK, :] = rows[:, c * wide : (c + 1) * wide]
        out_ref[whole * select * BLOCK :, i * rest : (i + 1) * rest] = rows[:, whole * wide :]


def pick_stored(stored, held_at, holding, wide):
    high = held_at.shape[0] * BLOCK * stored.shape[1] // wide
    return pl.pallas_call(
        pick_kernel,
        in_specs=[
            pl.BlockSpec(memory_space=pltpu.SMEM),
            pl.BlockSpec(memory_space=pltpu.SMEM),
            pl.BlockSpec(memory_space=pltpu.VMEM),
        ],
        out_specs=pl.BlockSpec(memory_space=pltpu.VMEM),
        out_shape=jax.ShapeDtypeStruct((high, wide), jnp.bfloat16),
        cost_estimate=pl.CostEstimate(
            flops=0, bytes_accessed=2 * (stored.size + high * wide), transcendentals=0
        ),
        compiler_params=pltpu.CompilerParams(vmem_limit_bytes=24 * MIB),
    )(held_at, holding.astype(jnp.int32), stored)


def restore_kernel(products_ref, packed_ref, out_ref):
    select, _, hidden = out_ref.shape
    wide = packed_ref.shape[1]
    whole = hidden // wide
    rest = hidden - whole * wide
    for i in range(select):
        at = slice(i * BLOCK, (i + 1) * BLOCK)
        for c in range(whole):
            start, columns = (c * select + i) * BLOCK, slice(c * wide, (c + 1) * wide)
            out_ref[i, :, columns] = products_ref[at, columns] + packed_ref[
                start : start + BLOCK, :
            ].astype(jnp.float32)
        out_ref[i, :, whole * wide :] = products_ref[at, whole * wide :] + packed_ref[
            whole * select * BLOCK :, i * rest : (i + 1) * rest
        ].astype(jnp.float32)


def add_stored(products, shown, at, select):
    hidden = products.shape[1]
    wide = shown.shape[1] // (at + 1)
    return pl.pallas_call(
        restore_kernel,
        grid=(1,),
        in_specs=[
            pl.BlockSpec((select * BLOCK, hidden), lambda i: (0, 0)),
            pl.BlockSpec((shown.shape[0], wide), lambda i: (0, at)),
        ],
        out_specs=pl.BlockSpec((select, BLOCK, hidden), lambda i: (0, 0, 0)),
        out_shape=jax.ShapeDtypeStruct((select, BLOCK, hidden), jnp.float32),
        cost_estimate=pl.CostEstimate(
            flops=select * BLOCK * hidden,
            bytes_accessed=10 * select * BLOCK * hidden,
            transcendentals=0,
        ),
        compiler_params=pltpu.CompilerParams(vmem_limit_bytes=32 * MIB),
    )(products, shown)


def hidden_kernel(weight_ref, rows_ref, *refs):
    out_ref, high = refs[-1], weight_ref.shape[0]
    out_ref[:high, :] = lax.dot_general(
        weight_ref[...],
        rows_ref[...],
        (((1,), (1,)), ((), ())),
        preferred_element_type=jnp.float32,
    ).astype(out_ref.dtype)
    if len(refs) > 1:
        out_ref[high:, :] = refs[0][...]


def hidden_product(weight, rows, extra, steps):
    high, depth = weight.shape
    slots = rows.shape[0]
    more = [] if extra is None else [extra]
    total = high + sum(e.shape[0] for e in more)
    return pl.pallas_call(
        hidden_kernel,
        grid=(steps,),
        in_specs=[
            pl.BlockSpec((high // steps, depth), lambda i: (i, 0)),
            pl.BlockSpec((slots, depth), lambda i: (0, 0)),
        ]
        + [pl.BlockSpec((e.shape[0] // steps, slots), lambda i: (i, 0)) for e in more],
        out_specs=pl.BlockSpec((total // steps, slots), lambda i: (i, 0)),
        out_shape=jax.ShapeDtypeStruct((total, slots), jnp.bfloat16),
        cost_estimate=pl.CostEstimate(
            flops=2 * high * depth * slots,
            bytes_accessed=2 * (high * depth + slots * depth + 2 * total * slots),
            transcendentals=0,
        ),
        compiler_params=pltpu.CompilerParams(vmem_limit_bytes=32 * MIB),
    )(weight, rows, *more)


def gates_kernel(rows_ref, grad_ref, *refs):
    weights, own_ref = refs[:-1], refs[-1]
    own_hidden, depth = own_ref.shape[0] // 2, weights[0].shape[1]
    slots = own_ref.shape[1]
    pre = None
    for d, weight in enumerate(weights):
        term = lax.dot_general(
            weight[...],
            rows_ref[:, :, :, d * depth : (d + 1) * depth].reshape(slots, depth),
            (((1,), (1,)), ((), ())),
            preferred_element_type=jnp.float32,
        )
        pre = term if pre is None else pre + term
    gate_pre, up_pre = pre[:own_hidden], pre[own_hidden:]
    hidden_grad = grad_ref[...].astype(jnp.float32)
    squashed = 1.0 / (1.0 + jnp.exp(-gate_pre))
    own_ref[:own_hidden, :] = (
        hidden_grad * up_pre * squashed * (1.0 + gate_pre * (1.0 - squashed))
    ).astype(own_ref.dtype)
    own_ref[own_hidden:, :] = (hidden_grad * gate_pre * squashed).astype(own_ref.dtype)


def hidden_gates(weights, rows, first, count, hidden_grad, at, tile):
    groups, _, low, width = rows.shape
    high, slots = weights[0].shape[0], groups * count * low
    own_hidden = high // 2
    block = (tile // (count * low), count, low, width)
    whole = pl.BlockSpec(weights[0].shape, lambda i: (0, 0))
    return pl.pallas_call(
        gates_kernel,
        grid=(slots // tile,),
        in_specs=[
            pl.BlockSpec(block, lambda i: (i, first // count, 0, 0)),
            pl.BlockSpec((own_hidden, tile), lambda i: (0, at + i)),
        ]
        + [whole] * len(weights),
        out_specs=pl.BlockSpec((high, tile), lambda i: (0, i)),
        out_shape=jax.ShapeDtypeStruct((high, slots), jnp.bfloat16),
        cost_estimate=pl.CostEstimate(
            flops=2 * high * width * slots,
            bytes_accessed=2 * (high * width + slots * width + 2 * high * slots),
            transcendentals=high // 2 * slots,
        ),
        compiler_params=pltpu.CompilerParams(vmem_limit_bytes=56 * MIB),
    )(rows, hidden_grad, *weights)


def part_kernel(own_ref, *refs):
    weights, out_ref = refs[:-1], refs[-1]
    depth = weights[0].shape[1]
    own = own_ref[...].T
    for d, weight in enumerate(weights):
        out_ref[:, d * depth : (d + 1) * depth] = jnp.dot(
            own, weight[...], preferred_element_type=jnp.float32
        ).astype(out_ref.dtype)


def slot_parts(own, weights, tile):
    high, slots = own.shape
    width = weights[0].shape[1] * len(weights)
    whole = pl.BlockSpec(weights[0].shape, lambda i: (0, 0))
    return pl.pallas_call(
        part_kernel,
        grid=(slots // tile,),
        in_specs=[pl.BlockSpec((high, tile), lambda i: (0, i))] + [whole] * len(weights),
        out_specs=pl.BlockSpec((tile, width), lambda i: (i, 0)),
        out_shape=jax.ShapeDtypeStruct((slots, width), jnp.bfloat16),
        cost_estimate=pl.CostEstimate(
            flops=2 * high * width * slots,
            bytes_accessed=2 * (high * width + slots * width + high * slots),
            transcendentals=0,
        ),
        compiler_params=pltpu.CompilerParams(vmem_limit_bytes=56 * MIB),
    )(own, *weights)


def combine_kernel(behind_ref, *refs):
    out_ref, half_refs = refs[-1], refs[:-1]
    sides, shares, half, features = out_ref.shape
    for q in range(shares):
        at = pl.ds(pl.multiple_of(behind_ref[q] * features, BLOCK), features)
        rows = jnp.zeros((sides * half, features), jnp.float32)
        for placing_ref, parts_ref in zip(half_refs[::2], half_refs[1::2]):
            rows = rows + jnp.dot(
                placing_ref[...], parts_ref[:, at], preferred_element_type=jnp.float32
            )
        rows = rows.astype(out_ref.dtype)
        for j in range(sides):
            out_ref[j, q] = rows[j * half : (j + 1) * half]


def combine(pairs, behind, sides):
    tok_rows = pairs[0][0].shape[0]
    width = pairs[0][1].shape[1]
    slots = sum(placing.shape[1] for placing, _ in pairs)
    shares = behind.shape[0]
    return pl.pallas_call(
        combine_kernel,
        in_specs=[pl.BlockSpec(memory_space=pltpu.SMEM)]
        + [pl.BlockSpec(memory_space=pltpu.VMEM)] * (2 * len(pairs)),
        out_specs=pl.BlockSpec(memory_space=pltpu.VMEM),
        out_shape=jax.ShapeDtypeStruct(
            (sides, shares, tok_rows // sides, width // shares), jnp.bfloat16
        ),
        cost_estimate=pl.CostEstimate(
            flops=2 * slots * tok_rows * width,
            bytes_accessed=2 * (slots * width + slots * tok_rows + tok_rows * width),
            transcendentals=0,
        ),
        compiler_params=pltpu.CompilerParams(vmem_limit_bytes=32 * MIB),
    )(behind, *[array for pair in pairs for array in pair])


def body(
    tokens,
    cotangent,
    gate_values,
    expert_ids,
    gate_weight,
    up_weight,
    down_weight,
    block_ids,
    feedback,
):
    groups = lax.axis_size("expert")
    shares = lax.axis_size("replica")
    sides = lax.axis_size("tensor")
    here = lax.axis_index("replica")
    experts = groups * gate_weight.shape[0]
    tok_rows, top_count = expert_ids.shape
    capacity = min(tok_rows, tok_rows * top_count * 3 // (2 * experts))
    features = tokens.shape[1]
    width = features * shares
    hidden = gate_weight.shape[2]
    own_hidden = hidden // shares
    stored = feedback[0]

    local_blocks = features // BLOCK
    local_ids = block_ids[0] - here * local_blocks
    holding = jnp.logical_and(local_ids >= 0, local_ids < local_blocks)
    held_at = jnp.clip(local_ids, 0, local_blocks - 1) * BLOCK
    select = local_ids.shape[0]

    pieces = split_weights(gate_weight[0], up_weight[0], here, shares)
    expert_ids, *pieces = lax.optimization_barrier((expert_ids, *pieces))

    def hand_out(d):
        return lax.ppermute(pieces[d], "replica", shift_by(d, shares))

    got = {d: hand_out(d) if d else pieces[0] for d in (0, 4, 3, 5, 2, 6, 1, 7)}

    padded = jnp.pad(tokens, ((0, SPARE), (0, 0)))
    gathered = lax.all_gather(padded, "replica", axis=0, tiled=False)

    low = capacity // 3
    lots = ((0, 1), (1, 1), (2, 1))
    lot_slots = [groups * count * low for _, count in lots]

    def lot_of(rows, lot):
        first, count = lots[lot]
        return rows[:, first * low : (first + count) * low].reshape(lot_slots[lot], -1)

    placing, slot_gate = routing_tables(expert_ids, gate_values, experts, capacity)
    sent_grads = (
        jnp.dot(placing, cotangent, preferred_element_type=jnp.float32) * slot_gate[:, None]
    ).astype(jnp.bfloat16)
    sent_grads = sent_grads.reshape(experts, capacity, features)
    stored_rows = pick_stored(stored, held_at, holding, lot_slots[2])
    sent_grads, stored_rows = lax.optimization_barrier((sent_grads, stored_rows))
    arrived_grads = lax.all_to_all(sent_grads, "expert", split_axis=0, concat_axis=0, tiled=True)
    w_down = down_weight[0]
    early = jnp.concatenate([lot_of(arrived_grads, 0), lot_of(arrived_grads, 1)], axis=0)
    hidden_first = hidden_product(w_down, early, None, shares)
    hidden_first, got[4] = lax.optimization_barrier((hidden_first, got[4]))
    hidden_second = hidden_product(w_down, lot_of(arrived_grads, 2), stored_rows, shares)
    grads_first = lax.psum_scatter(hidden_first, "replica", scatter_dimension=0, tiled=True)

    behind = (here - jnp.arange(shares, dtype=jnp.int32)) % shares
    whole_tokens = jnp.take(gathered[:, :tok_rows], behind, axis=0)
    whole_tokens = whole_tokens.transpose(1, 0, 2).reshape(tok_rows, width)
    sent_rows = jnp.dot(placing, whole_tokens, preferred_element_type=jnp.float32)
    sent_rows = sent_rows.astype(jnp.bfloat16).reshape(experts, capacity, width)
    sent_rows, hidden_second, got[1], got[7] = lax.optimization_barrier(
        (sent_rows, hidden_second, got[1], got[7])
    )
    arrived = lax.all_to_all(sent_rows, "expert", split_axis=0, concat_axis=0, tiled=True)
    hidden_second, arrived, *weights = lax.optimization_barrier(
        (hidden_second, arrived, *[got[d] for d in range(shares)])
    )
    grads_second = lax.psum_scatter(hidden_second, "replica", scatter_dimension=0, tiled=True)

    def give_back(parts):
        parts = parts.reshape(experts, -1, width)
        back = lax.all_to_all(parts, "expert", split_axis=0, concat_axis=0, tiled=True)
        return back.reshape(-1, width)

    tiles = arrived.reshape(groups, capacity // low, low, width)
    tile = lot_slots[0]
    own, parts, back = {}, {}, {}
    for lot in (0, 1):
        own[lot] = hidden_gates(weights, tiles, *lots[lot], grads_first, lot, tile)
        parts[lot] = slot_parts(own[lot], weights, tile)
    back[0] = give_back(parts[0])
    grads_second, parts[1], back[0] = lax.optimization_barrier((grads_second, parts[1], back[0]))
    back[1] = give_back(parts[1])
    own[2] = hidden_gates(weights, tiles, *lots[2], grads_second[:own_hidden], 0, tile)
    parts[2] = slot_parts(own[2], weights, tile)
    parts[2], back[1] = lax.optimization_barrier((parts[2], back[1]))
    back[2] = give_back(parts[2])

    shown = jnp.concatenate(
        [own[lot][:own_hidden] for lot in range(3)] + [grads_second[own_hidden:]], axis=1
    )
    shown = lax.all_gather(shown, "replica", axis=0, tiled=True)
    slots = sum(lot_slots)
    placed = (here - block_ids[0] // local_blocks) % shares
    picked_at = placed * features + block_ids[0] % local_blocks * BLOCK
    wanted = jnp.concatenate(
        [
            lax.dynamic_slice_in_dim(arrived, picked_at[i], BLOCK, axis=2)
            for i in range(select)
        ]
        + [arrived[:, :, :features]],
        axis=2,
    )
    wanted = jnp.concatenate([lot_of(wanted, lot) for lot in range(3)], axis=0)
    wanted = jnp.pad(wanted, ((0, shown.shape[1] - slots), (0, 0)))
    wanted, shown = lax.optimization_barrier((wanted, shown))
    products = jnp.einsum("sd,fs->df", wanted, shown, preferred_element_type=jnp.float32)
    block_sums = add_stored(products, shown, slots // tile, select)
    gradient = products[select * BLOCK :] + stored.astype(jnp.float32)
    struck = jnp.any(
        local_ids[:, None] == jnp.arange(local_blocks, dtype=jnp.int32)[None, :], axis=0
    )
    retained = (
        jnp.where(
            struck[:, None, None],
            jnp.float32(0.0),
            gradient.reshape(local_blocks, BLOCK, hidden),
        )
        .reshape(gradient.shape)
        .astype(jnp.bfloat16)
    )

    placing = placing.reshape(experts, capacity, tok_rows)
    combined = combine(
        [(lot_of(placing, lot).T, back[lot]) for lot in range(3)], behind, sides
    )
    combined = combined.reshape(sides * shares, tok_rows // sides, features)
    collected = lax.all_to_all(
        combined, ("tensor", "replica"), split_axis=0, concat_axis=0, tiled=True
    )
    collected, retained, block_sums = lax.optimization_barrier((collected, retained, block_sums))
    token_grad = jnp.sum(collected.astype(jnp.float32), axis=0).astype(jnp.bfloat16)
    return (token_grad, block_sums[None], retained[None])


def solution(mesh):
    return jax.shard_map(
        body,
        mesh=mesh,
        in_specs=(
            P("expert", "replica"),
            P("expert", "replica"),
            P("expert", None),
            P("expert", None),
            P("expert", "replica", "tensor"),
            P("expert", "replica", "tensor"),
            P("expert", "tensor", "replica"),
            P("expert", None),
            P("expert", "replica", "tensor"),
        ),
        out_specs=(
            P(("expert", "tensor"), "replica"),
            P("expert", None, None, "tensor"),
            P("expert", "replica", "tensor"),
        ),
        check_vma=False,
    )
```

```python
import jax
import jax.numpy as jnp
from jax import lax
from jax.experimental import pallas as pl
from jax.experimental.pallas import tpu as pltpu
from jax.sharding import PartitionSpec as P

BLOCK = 128


def routing_tables(expert_ids, gate_values, experts, capacity):
    tok_rows, top_count = expert_ids.shape
    flat_ids = expert_ids.reshape(-1)
    choose = (flat_ids[:, None] == jnp.arange(experts, dtype=jnp.int32)[None, :]).astype(jnp.int32)
    before = jnp.cumsum(choose, axis=0) - choose
    slot_index = jnp.sum(before * choose, axis=1)
    target = (flat_ids * capacity + slot_index).reshape(tok_rows, top_count)
    matches = target[None, :, :] == jnp.arange(experts * capacity, dtype=jnp.int32)[:, None, None]
    placing = jnp.any(matches, axis=2).astype(jnp.bfloat16)
    slot_gate = jnp.sum(jnp.where(matches, gate_values[None, :, :], jnp.float32(0.0)), axis=(1, 2))
    return (placing, slot_gate)


MIB = 1024 * 1024
SPARE = 48


def shift_by(distance, size):
    return [(i, (i + distance) % size) for i in range(size)]


def split_kernel(own_hidden, here_ref, gate_ref, up_ref, *refs):
    outs, turned = refs[:-1], refs[-1]
    columns = gate_ref.shape[1]

    @pl.loop(0, columns // BLOCK)
    def _(tile):
        at = pl.ds(pl.multiple_of(tile * BLOCK, BLOCK), BLOCK)
        turned[0, at, :] = gate_ref[:, at].T
        turned[1, at, :] = up_ref[:, at].T

    for d, out in enumerate(outs):
        owner = lax.rem(here_ref[0] + d, len(outs))
        rows = pl.ds(pl.multiple_of(owner * own_hidden, 16), own_hidden)
        out[:own_hidden, :] = turned[0, rows, :]
        out[own_hidden:, :] = turned[1, rows, :]


def split_weights(w_gate, w_up, here, shares):
    features, hidden = w_gate.shape
    own_hidden = hidden // shares
    piece = jax.ShapeDtypeStruct((2 * own_hidden, features), jnp.bfloat16)
    return pl.pallas_call(
        lambda *refs: split_kernel(own_hidden, *refs),
        in_specs=[
            pl.BlockSpec(memory_space=pltpu.SMEM),
            pl.BlockSpec(memory_space=pltpu.VMEM),
            pl.BlockSpec(memory_space=pltpu.VMEM),
        ],
        out_specs=[pl.BlockSpec(memory_space=pltpu.VMEM)] * shares,
        out_shape=[piece] * shares,
        scratch_shapes=[pltpu.VMEM((2, hidden, features), jnp.bfloat16)],
        cost_estimate=pl.CostEstimate(
            flops=0, bytes_accessed=8 * hidden * features, transcendentals=0
        ),
        compiler_params=pltpu.CompilerParams(vmem_limit_bytes=58 * MIB),
    )(here.reshape(1), w_gate, w_up)


def pick_kernel(at_ref, holds_ref, stored_ref, out_ref):
    wide, select = out_ref.shape[1], at_ref.shape[0]
    whole = stored_ref.shape[1] // wide
    rest = stored_ref.shape[1] - whole * wide
    for i in range(select):
        rows = stored_ref[pl.ds(pl.multiple_of(at_ref[i], BLOCK), BLOCK), :]
        rows = jnp.where(holds_ref[i] > 0, rows, jnp.zeros_like(rows))
        for c in range(whole):
            start = (c * select + i) * BLOCK
            out_ref[start : start + BLOCK, :] = rows[:, c * wide : (c + 1) * wide]
        out_ref[whole * select * BLOCK :, i * rest : (i + 1) * rest] = rows[:, whole * wide :]


def pick_stored(stored, held_at, holding, wide):
    high = held_at.shape[0] * BLOCK * stored.shape[1] // wide
    return pl.pallas_call(
        pick_kernel,
        in_specs=[
            pl.BlockSpec(memory_space=pltpu.SMEM),
            pl.BlockSpec(memory_space=pltpu.SMEM),
            pl.BlockSpec(memory_space=pltpu.VMEM),
        ],
        out_specs=pl.BlockSpec(memory_space=pltpu.VMEM),
        out_shape=jax.ShapeDtypeStruct((high, wide), jnp.bfloat16),
        cost_estimate=pl.CostEstimate(
            flops=0, bytes_accessed=2 * (stored.size + high * wide), transcendentals=0
        ),
        compiler_params=pltpu.CompilerParams(vmem_limit_bytes=24 * MIB),
    )(held_at, holding.astype(jnp.int32), stored)


def restore_kernel(products_ref, packed_ref, out_ref):
    select, _, hidden = out_ref.shape
    wide = packed_ref.shape[1]
    whole = hidden // wide
    rest = hidden - whole * wide
    for i in range(select):
        at = slice(i * BLOCK, (i + 1) * BLOCK)
        for c in range(whole):
            start, columns = (c * select + i) * BLOCK, slice(c * wide, (c + 1) * wide)
            out_ref[i, :, columns] = products_ref[at, columns] + packed_ref[
                start : start + BLOCK, :
            ].astype(jnp.float32)
        out_ref[i, :, whole * wide :] = products_ref[at, whole * wide :] + packed_ref[
            whole * select * BLOCK :, i * rest : (i + 1) * rest
        ].astype(jnp.float32)


def add_stored(products, shown, at, select):
    hidden = products.shape[1]
    wide = shown.shape[1] // (at + 1)
    return pl.pallas_call(
        restore_kernel,
        grid=(1,),
        in_specs=[
            pl.BlockSpec((select * BLOCK, hidden), lambda i: (0, 0)),
            pl.BlockSpec((shown.shape[0], wide), lambda i: (0, at)),
        ],
        out_specs=pl.BlockSpec((select, BLOCK, hidden), lambda i: (0, 0, 0)),
        out_shape=jax.ShapeDtypeStruct((select, BLOCK, hidden), jnp.float32),
        cost_estimate=pl.CostEstimate(
            flops=select * BLOCK * hidden,
            bytes_accessed=10 * select * BLOCK * hidden,
            transcendentals=0,
        ),
        compiler_params=pltpu.CompilerParams(vmem_limit_bytes=32 * MIB),
    )(products, shown)


def hidden_kernel(weight_ref, rows_ref, *refs):
    out_ref, high = refs[-1], weight_ref.shape[0]
    out_ref[:high, :] = lax.dot_general(
        weight_ref[...],
        rows_ref[...],
        (((1,), (1,)), ((), ())),
        preferred_element_type=jnp.float32,
    ).astype(out_ref.dtype)
    if len(refs) > 1:
        out_ref[high:, :] = refs[0][...]


def hidden_product(weight, rows, extra, steps):
    high, depth = weight.shape
    slots = rows.shape[0]
    more = [] if extra is None else [extra]
    total = high + sum(e.shape[0] for e in more)
    return pl.pallas_call(
        hidden_kernel,
        grid=(steps,),
        in_specs=[
            pl.BlockSpec((high // steps, depth), lambda i: (i, 0)),
            pl.BlockSpec((slots, depth), lambda i: (0, 0)),
        ]
        + [pl.BlockSpec((e.shape[0] // steps, slots), lambda i: (i, 0)) for e in more],
        out_specs=pl.BlockSpec((total // steps, slots), lambda i: (i, 0)),
        out_shape=jax.ShapeDtypeStruct((total, slots), jnp.bfloat16),
        cost_estimate=pl.CostEstimate(
            flops=2 * high * depth * slots,
            bytes_accessed=2 * (high * depth + slots * depth + 2 * total * slots),
            transcendentals=0,
        ),
        compiler_params=pltpu.CompilerParams(vmem_limit_bytes=32 * MIB),
    )(weight, rows, *more)


def gates_kernel(shares, rows_ref, grad_ref, *refs):
    weights, others = refs[:shares], refs[shares:]
    own_hidden, depth = grad_ref.shape[0], weights[0].shape[1]
    slots = grad_ref.shape[1]
    pre = None
    for d, weight in enumerate(weights):
        term = lax.dot_general(
            weight[...],
            rows_ref[:, :, :, d * depth : (d + 1) * depth].reshape(slots, depth),
            (((1,), (1,)), ((), ())),
            preferred_element_type=jnp.float32,
        )
        pre = term if pre is None else pre + term
    gate_pre, up_pre = pre[:own_hidden], pre[own_hidden:]
    hidden_grad = grad_ref[...].astype(jnp.float32)
    squashed = 1.0 / (1.0 + jnp.exp(-gate_pre))
    grad_gate = (hidden_grad * up_pre * squashed * (1.0 + gate_pre * (1.0 - squashed))).astype(
        jnp.bfloat16
    )
    grad_up = (hidden_grad * gate_pre * squashed).astype(jnp.bfloat16)
    own_ref = others[-1]
    at = own_ref.shape[1] - slots
    own_ref[:own_hidden, at:] = grad_gate
    own_ref[own_hidden:, at:] = grad_up
    if len(others) > 1:
        first_ref, second_ref, extra_ref, shown_ref, _ = others
        own_ref[:, :at] = second_ref[...]
        for lot, rows in enumerate(
            (first_ref[...], second_ref[:own_hidden, :], grad_gate, extra_ref[...])
        ):
            shown_ref[:, lot * slots : (lot + 1) * slots] = rows


def hidden_gates(weights, rows, lot, hidden_grad, at, earlier=()):
    groups, _, low, width = rows.shape
    high, slots = weights[0].shape[0], groups * low
    own_hidden = high // 2
    wide = 2 * slots if earlier else slots
    out_shape = [jax.ShapeDtypeStruct((high, wide), jnp.bfloat16)]
    in_specs = [
        pl.BlockSpec((groups, 1, low, width), lambda i: (0, lot, 0, 0)),
        pl.BlockSpec((own_hidden, slots), lambda i: (0, at)),
    ] + [pl.BlockSpec(weights[0].shape, lambda i: (0, 0))] * len(weights)
    operands = [rows, hidden_grad, *weights]
    if earlier:
        in_specs += [
            pl.BlockSpec((own_hidden, slots), lambda i: (0, 0)),
            pl.BlockSpec((high, slots), lambda i: (0, 0)),
            pl.BlockSpec((own_hidden, slots), lambda i: (1, 0)),
        ]
        operands += [*earlier, hidden_grad]
        out_shape.insert(0, jax.ShapeDtypeStruct((own_hidden, 4 * slots), jnp.bfloat16))
    out_specs = [pl.BlockSpec(o.shape, lambda i: (0, 0)) for o in out_shape]
    return pl.pallas_call(
        lambda *refs: gates_kernel(len(weights), *refs),
        grid=(1,),
        in_specs=in_specs,
        out_specs=out_specs,
        out_shape=out_shape,
        cost_estimate=pl.CostEstimate(
            flops=2 * high * width * slots,
            bytes_accessed=2 * (high * width + slots * width + 2 * high * slots),
            transcendentals=own_hidden * slots,
        ),
        compiler_params=pltpu.CompilerParams(vmem_limit_bytes=56 * MIB),
    )(*operands)


def part_kernel(own_ref, *refs):
    weights, out_ref = refs[:-1], refs[-1]
    groups, _, low, _ = out_ref.shape
    depth = weights[0].shape[1]
    own = own_ref[...].T
    for d, weight in enumerate(weights):
        out_ref[:, 0, :, d * depth : (d + 1) * depth] = (
            jnp.dot(own, weight[...], preferred_element_type=jnp.float32)
            .astype(out_ref.dtype)
            .reshape(groups, low, depth)
        )


def slot_parts(own, weights, groups, low):
    high, slots = own.shape
    lots = slots // (groups * low)
    width = weights[0].shape[1] * len(weights)
    whole = pl.BlockSpec(weights[0].shape, lambda i: (0, 0))
    return pl.pallas_call(
        part_kernel,
        grid=(lots,),
        in_specs=[pl.BlockSpec((high, groups * low), lambda i: (0, i))] + [whole] * len(weights),
        out_specs=pl.BlockSpec((groups, 1, low, width), lambda i: (0, i, 0, 0)),
        out_shape=jax.ShapeDtypeStruct((groups, lots, low, width), jnp.bfloat16),
        cost_estimate=pl.CostEstimate(
            flops=2 * high * width * slots,
            bytes_accessed=2 * (high * width + slots * width + high * slots),
            transcendentals=0,
        ),
        compiler_params=pltpu.CompilerParams(vmem_limit_bytes=56 * MIB),
    )(own, *weights)


def combine_kernel(behind_ref, *refs):
    out_ref, half_refs = refs[-1], refs[:-1]
    sides, shares, half, features = out_ref.shape
    for q in range(shares):
        at = pl.ds(pl.multiple_of(behind_ref[q] * features, BLOCK), features)
        rows = jnp.zeros((sides * half, features), jnp.float32)
        for placing_ref, parts_ref in zip(half_refs[::2], half_refs[1::2]):
            rows = rows + jnp.dot(
                placing_ref[...], parts_ref[:, at], preferred_element_type=jnp.float32
            )
        rows = rows.astype(out_ref.dtype)
        for j in range(sides):
            out_ref[j, q] = rows[j * half : (j + 1) * half]


def combine(pairs, behind, sides):
    tok_rows = pairs[0][0].shape[0]
    width = pairs[0][1].shape[1]
    slots = sum(placing.shape[1] for placing, _ in pairs)
    shares = behind.shape[0]
    return pl.pallas_call(
        combine_kernel,
        in_specs=[pl.BlockSpec(memory_space=pltpu.SMEM)]
        + [pl.BlockSpec(memory_space=pltpu.VMEM)] * (2 * len(pairs)),
        out_specs=pl.BlockSpec(memory_space=pltpu.VMEM),
        out_shape=jax.ShapeDtypeStruct(
            (sides, shares, tok_rows // sides, width // shares), jnp.bfloat16
        ),
        cost_estimate=pl.CostEstimate(
            flops=2 * slots * tok_rows * width,
            bytes_accessed=2 * (slots * width + slots * tok_rows + tok_rows * width),
            transcendentals=0,
        ),
        compiler_params=pltpu.CompilerParams(vmem_limit_bytes=32 * MIB),
    )(behind, *[array for pair in pairs for array in pair])


def body(
    tokens,
    cotangent,
    gate_values,
    expert_ids,
    gate_weight,
    up_weight,
    down_weight,
    block_ids,
    feedback,
):
    groups = lax.axis_size("expert")
    shares = lax.axis_size("replica")
    sides = lax.axis_size("tensor")
    here = lax.axis_index("replica")
    experts = groups * gate_weight.shape[0]
    tok_rows, top_count = expert_ids.shape
    capacity = min(tok_rows, tok_rows * top_count * 3 // (2 * experts))
    features = tokens.shape[1]
    width = features * shares
    hidden = gate_weight.shape[2]
    own_hidden = hidden // shares
    stored = feedback[0]

    local_blocks = features // BLOCK
    local_ids = block_ids[0] - here * local_blocks
    holding = jnp.logical_and(local_ids >= 0, local_ids < local_blocks)
    held_at = jnp.clip(local_ids, 0, local_blocks - 1) * BLOCK
    select = local_ids.shape[0]

    pieces = split_weights(gate_weight[0], up_weight[0], here, shares)
    expert_ids, *pieces = lax.optimization_barrier((expert_ids, *pieces))

    def hand_out(d):
        return lax.ppermute(pieces[d], "replica", shift_by(d, shares))

    got = {d: hand_out(d) if d else pieces[0] for d in (0, 4, 3, 5, 2, 6, 1, 7)}

    padded = jnp.pad(tokens, ((0, SPARE), (0, 0)))
    gathered = lax.all_gather(padded, "replica", axis=0, tiled=False)

    low = capacity // 3
    lots = ((0, 1), (1, 1), (2, 1))
    lot_slots = [groups * count * low for _, count in lots]

    def lot_of(rows, lot):
        first, count = lots[lot]
        return rows[:, first * low : (first + count) * low].reshape(lot_slots[lot], -1)

    placing, slot_gate = routing_tables(expert_ids, gate_values, experts, capacity)
    sent_grads = (
        jnp.dot(placing, cotangent, preferred_element_type=jnp.float32) * slot_gate[:, None]
    ).astype(jnp.bfloat16)
    sent_grads = sent_grads.reshape(experts, capacity, features)
    stored_rows = pick_stored(stored, held_at, holding, lot_slots[2])
    sent_grads, stored_rows = lax.optimization_barrier((sent_grads, stored_rows))
    arrived_grads = lax.all_to_all(sent_grads, "expert", split_axis=0, concat_axis=0, tiled=True)
    w_down = down_weight[0]
    early = jnp.concatenate([lot_of(arrived_grads, 0), lot_of(arrived_grads, 1)], axis=0)
    hidden_first = hidden_product(w_down, early, None, shares)
    hidden_first, got[4] = lax.optimization_barrier((hidden_first, got[4]))
    hidden_second = hidden_product(w_down, lot_of(arrived_grads, 2), stored_rows, shares)
    grads_first = lax.psum_scatter(hidden_first, "replica", scatter_dimension=0, tiled=True)

    behind = (here - jnp.arange(shares, dtype=jnp.int32)) % shares
    whole_tokens = jnp.take(gathered[:, :tok_rows], behind, axis=0)
    whole_tokens = whole_tokens.transpose(1, 0, 2).reshape(tok_rows, width)
    sent_rows = jnp.dot(placing, whole_tokens, preferred_element_type=jnp.float32)
    sent_rows = sent_rows.astype(jnp.bfloat16).reshape(experts, capacity, width)
    sent_rows, hidden_second, got[1], got[7] = lax.optimization_barrier(
        (sent_rows, hidden_second, got[1], got[7])
    )
    arrived = lax.all_to_all(sent_rows, "expert", split_axis=0, concat_axis=0, tiled=True)
    hidden_second, arrived, *weights = lax.optimization_barrier(
        (hidden_second, arrived, *[got[d] for d in range(shares)])
    )
    grads_second = lax.psum_scatter(hidden_second, "replica", scatter_dimension=0, tiled=True)

    def give_back(parts):
        parts = parts.reshape(experts, -1, width)
        back = lax.all_to_all(parts, "expert", split_axis=0, concat_axis=0, tiled=True)
        return back.reshape(-1, width)

    tiles = arrived.reshape(groups, capacity // low, low, width)
    tile = lot_slots[0]
    (first,) = hidden_gates(weights, tiles, 0, grads_first, 0)
    back_first = give_back(slot_parts(first, weights, groups, low))
    (second,) = hidden_gates(weights, tiles, 1, grads_first, 1)
    grads_second, second, back_first = lax.optimization_barrier(
        (grads_second, second, back_first)
    )
    shown, later = hidden_gates(weights, tiles, 2, grads_second, 0, (first, second))
    back_later = give_back(slot_parts(later, weights, groups, low))

    shown = lax.all_gather(shown, "replica", axis=0, tiled=True)
    slots = sum(lot_slots)
    placed = (here - block_ids[0] // local_blocks) % shares
    picked_at = placed * features + block_ids[0] % local_blocks * BLOCK
    wanted = jnp.concatenate(
        [
            lax.dynamic_slice_in_dim(arrived, picked_at[i], BLOCK, axis=2)
            for i in range(select)
        ]
        + [arrived[:, :, :features]],
        axis=2,
    )
    wanted = jnp.concatenate([lot_of(wanted, lot) for lot in range(3)], axis=0)
    wanted = jnp.pad(wanted, ((0, shown.shape[1] - slots), (0, 0)))
    wanted, shown = lax.optimization_barrier((wanted, shown))
    products = jnp.einsum("sd,fs->df", wanted, shown, preferred_element_type=jnp.float32)
    block_sums = add_stored(products, shown, slots // tile, select)
    gradient = products[select * BLOCK :] + stored.astype(jnp.float32)
    struck = jnp.any(
        local_ids[:, None] == jnp.arange(local_blocks, dtype=jnp.int32)[None, :], axis=0
    )
    retained = (
        jnp.where(
            struck[:, None, None],
            jnp.float32(0.0),
            gradient.reshape(local_blocks, BLOCK, hidden),
        )
        .reshape(gradient.shape)
        .astype(jnp.bfloat16)
    )

    placing = placing.reshape(experts, capacity, tok_rows)
    placing_first = placing[:, :low].reshape(-1, tok_rows).T
    placing_later = placing[:, low:].reshape(-1, tok_rows).T
    combined = combine(
        [(placing_first, back_first), (placing_later, back_later)], behind, sides
    )
    combined = combined.reshape(sides * shares, tok_rows // sides, features)
    collected = lax.all_to_all(
        combined, ("tensor", "replica"), split_axis=0, concat_axis=0, tiled=True
    )
    collected, retained, block_sums = lax.optimization_barrier((collected, retained, block_sums))
    token_grad = jnp.sum(collected.astype(jnp.float32), axis=0).astype(jnp.bfloat16)
    return (token_grad, block_sums[None], retained[None])


def solution(mesh):
    return jax.shard_map(
        body,
        mesh=mesh,
        in_specs=(
            P("expert", "replica"),
            P("expert", "replica"),
            P("expert", None),
            P("expert", None),
            P("expert", "replica", "tensor"),
            P("expert", "replica", "tensor"),
            P("expert", "tensor", "replica"),
            P("expert", None),
            P("expert", "replica", "tensor"),
        ),
        out_specs=(
            P(("expert", "tensor"), "replica"),
            P("expert", None, None, "tensor"),
            P("expert", "replica", "tensor"),
        ),
        check_vma=False,
    )
```

```python
import jax
import jax.numpy as jnp
from jax import lax
from jax.experimental import pallas as pl
from jax.experimental.pallas import tpu as pltpu
from jax.sharding import PartitionSpec as P

BLOCK = 128


def routing_tables(expert_ids, gate_values, experts, capacity):
    tok_rows, top_count = expert_ids.shape
    flat_ids = expert_ids.reshape(-1)
    choose = (flat_ids[:, None] == jnp.arange(experts, dtype=jnp.int32)[None, :]).astype(jnp.int32)
    before = jnp.cumsum(choose, axis=0) - choose
    slot_index = jnp.sum(before * choose, axis=1)
    target = (flat_ids * capacity + slot_index).reshape(tok_rows, top_count)
    matches = target[None, :, :] == jnp.arange(experts * capacity, dtype=jnp.int32)[:, None, None]
    placing = jnp.any(matches, axis=2).astype(jnp.bfloat16)
    slot_gate = jnp.sum(jnp.where(matches, gate_values[None, :, :], jnp.float32(0.0)), axis=(1, 2))
    return (placing, slot_gate)


MIB = 1024 * 1024
SPARE = 48


def shift_by(distance, size):
    return [(i, (i + distance) % size) for i in range(size)]


def split_kernel(own_hidden, here_ref, gate_ref, up_ref, *refs):
    outs, turned = refs[:-1], refs[-1]
    columns = gate_ref.shape[1]

    @pl.loop(0, columns // BLOCK)
    def _(tile):
        at = pl.ds(pl.multiple_of(tile * BLOCK, BLOCK), BLOCK)
        turned[0, at, :] = gate_ref[:, at].T
        turned[1, at, :] = up_ref[:, at].T

    for d, out in enumerate(outs):
        owner = lax.rem(here_ref[0] + d, len(outs))
        rows = pl.ds(pl.multiple_of(owner * own_hidden, 16), own_hidden)
        out[:own_hidden, :] = turned[0, rows, :]
        out[own_hidden:, :] = turned[1, rows, :]


def split_weights(w_gate, w_up, here, shares):
    features, hidden = w_gate.shape
    own_hidden = hidden // shares
    piece = jax.ShapeDtypeStruct((2 * own_hidden, features), jnp.bfloat16)
    return pl.pallas_call(
        lambda *refs: split_kernel(own_hidden, *refs),
        in_specs=[
            pl.BlockSpec(memory_space=pltpu.SMEM),
            pl.BlockSpec(memory_space=pltpu.VMEM),
            pl.BlockSpec(memory_space=pltpu.VMEM),
        ],
        out_specs=[pl.BlockSpec(memory_space=pltpu.VMEM)] * shares,
        out_shape=[piece] * shares,
        scratch_shapes=[pltpu.VMEM((2, hidden, features), jnp.bfloat16)],
        cost_estimate=pl.CostEstimate(
            flops=0, bytes_accessed=8 * hidden * features, transcendentals=0
        ),
        compiler_params=pltpu.CompilerParams(vmem_limit_bytes=58 * MIB),
    )(here.reshape(1), w_gate, w_up)


def pick_kernel(at_ref, holds_ref, stored_ref, out_ref):
    wide, select = out_ref.shape[1], at_ref.shape[0]
    whole = stored_ref.shape[1] // wide
    rest = stored_ref.shape[1] - whole * wide
    for i in range(select):
        rows = stored_ref[pl.ds(pl.multiple_of(at_ref[i], BLOCK), BLOCK), :]
        rows = jnp.where(holds_ref[i] > 0, rows, jnp.zeros_like(rows))
        for c in range(whole):
            start = (c * select + i) * BLOCK
            out_ref[start : start + BLOCK, :] = rows[:, c * wide : (c + 1) * wide]
        out_ref[whole * select * BLOCK :, i * rest : (i + 1) * rest] = rows[:, whole * wide :]


def pick_stored(stored, held_at, holding, wide):
    high = held_at.shape[0] * BLOCK * stored.shape[1] // wide
    return pl.pallas_call(
        pick_kernel,
        in_specs=[
            pl.BlockSpec(memory_space=pltpu.SMEM),
            pl.BlockSpec(memory_space=pltpu.SMEM),
            pl.BlockSpec(memory_space=pltpu.VMEM),
        ],
        out_specs=pl.BlockSpec(memory_space=pltpu.VMEM),
        out_shape=jax.ShapeDtypeStruct((high, wide), jnp.bfloat16),
        cost_estimate=pl.CostEstimate(
            flops=0, bytes_accessed=2 * (stored.size + high * wide), transcendentals=0
        ),
        compiler_params=pltpu.CompilerParams(vmem_limit_bytes=24 * MIB),
    )(held_at, holding.astype(jnp.int32), stored)


def restore_kernel(products_ref, packed_ref, out_ref):
    select, _, hidden = out_ref.shape
    wide = packed_ref.shape[1]
    whole = hidden // wide
    rest = hidden - whole * wide
    for i in range(select):
        at = slice(i * BLOCK, (i + 1) * BLOCK)
        for c in range(whole):
            start, columns = (c * select + i) * BLOCK, slice(c * wide, (c + 1) * wide)
            out_ref[i, :, columns] = products_ref[at, columns] + packed_ref[
                start : start + BLOCK, :
            ].astype(jnp.float32)
        out_ref[i, :, whole * wide :] = products_ref[at, whole * wide :] + packed_ref[
            whole * select * BLOCK :, i * rest : (i + 1) * rest
        ].astype(jnp.float32)


def add_stored(products, shown, at, select):
    hidden = products.shape[1]
    wide = shown.shape[1] // (at + 1)
    return pl.pallas_call(
        restore_kernel,
        grid=(1,),
        in_specs=[
            pl.BlockSpec((select * BLOCK, hidden), lambda i: (0, 0)),
            pl.BlockSpec((shown.shape[0], wide), lambda i: (0, at)),
        ],
        out_specs=pl.BlockSpec((select, BLOCK, hidden), lambda i: (0, 0, 0)),
        out_shape=jax.ShapeDtypeStruct((select, BLOCK, hidden), jnp.float32),
        cost_estimate=pl.CostEstimate(
            flops=select * BLOCK * hidden,
            bytes_accessed=10 * select * BLOCK * hidden,
            transcendentals=0,
        ),
        compiler_params=pltpu.CompilerParams(vmem_limit_bytes=32 * MIB),
    )(products, shown)


def hidden_kernel(weight_ref, rows_ref, *refs):
    out_ref, high = refs[-1], weight_ref.shape[0]
    out_ref[:high, :] = lax.dot_general(
        weight_ref[...],
        rows_ref[...],
        (((1,), (1,)), ((), ())),
        preferred_element_type=jnp.float32,
    ).astype(out_ref.dtype)
    if len(refs) > 1:
        out_ref[high:, :] = refs[0][...]


def hidden_product(weight, rows, extra, steps):
    high, depth = weight.shape
    slots = rows.shape[0]
    more = [] if extra is None else [extra]
    total = high + sum(e.shape[0] for e in more)
    return pl.pallas_call(
        hidden_kernel,
        grid=(steps,),
        in_specs=[
            pl.BlockSpec((high // steps, depth), lambda i: (i, 0)),
            pl.BlockSpec((slots, depth), lambda i: (0, 0)),
        ]
        + [pl.BlockSpec((e.shape[0] // steps, slots), lambda i: (i, 0)) for e in more],
        out_specs=pl.BlockSpec((total // steps, slots), lambda i: (i, 0)),
        out_shape=jax.ShapeDtypeStruct((total, slots), jnp.bfloat16),
        cost_estimate=pl.CostEstimate(
            flops=2 * high * depth * slots,
            bytes_accessed=2 * (high * depth + slots * depth + 2 * total * slots),
            transcendentals=0,
        ),
        compiler_params=pltpu.CompilerParams(vmem_limit_bytes=32 * MIB),
    )(weight, rows, *more)


def gates_kernel(shares, rows_ref, grad_ref, *refs):
    weights, others = refs[:shares], refs[shares:]
    own_hidden, depth = grad_ref.shape[0], weights[0].shape[1]
    slots = grad_ref.shape[1]
    pre = None
    for d, weight in enumerate(weights):
        term = lax.dot_general(
            weight[...],
            rows_ref[:, :, :, d * depth : (d + 1) * depth].reshape(slots, depth),
            (((1,), (1,)), ((), ())),
            preferred_element_type=jnp.float32,
        )
        pre = term if pre is None else pre + term
    gate_pre, up_pre = pre[:own_hidden], pre[own_hidden:]
    hidden_grad = grad_ref[...].astype(jnp.float32)
    squashed = 1.0 / (1.0 + jnp.exp(-gate_pre))
    grad_gate = (hidden_grad * up_pre * squashed * (1.0 + gate_pre * (1.0 - squashed))).astype(
        jnp.bfloat16
    )
    grad_up = (hidden_grad * gate_pre * squashed).astype(jnp.bfloat16)
    own_ref = others[-1]
    own_ref[:own_hidden, :] = grad_gate
    own_ref[own_hidden:, :] = grad_up
    if len(others) > 1:
        first_ref, second_ref, extra_ref, shown_ref, _ = others
        for lot, rows in enumerate((first_ref[...], second_ref[...], grad_gate, extra_ref[...])):
            shown_ref[:, lot * slots : (lot + 1) * slots] = rows


def hidden_gates(weights, rows, lot, hidden_grad, at, earlier=()):
    groups, _, low, width = rows.shape
    high, slots = weights[0].shape[0], groups * low
    own_hidden = high // 2
    out_shape = [jax.ShapeDtypeStruct((high, slots), jnp.bfloat16)]
    in_specs = [
        pl.BlockSpec((groups, 1, low, width), lambda i: (0, lot, 0, 0)),
        pl.BlockSpec((own_hidden, slots), lambda i: (0, at)),
    ] + [pl.BlockSpec(weights[0].shape, lambda i: (0, 0))] * len(weights)
    operands = [rows, hidden_grad, *weights]
    if earlier:
        in_specs += [
            pl.BlockSpec((own_hidden, slots), lambda i: (0, 0)),
            pl.BlockSpec((own_hidden, slots), lambda i: (0, 0)),
            pl.BlockSpec((own_hidden, slots), lambda i: (1, 0)),
        ]
        operands += [*earlier, hidden_grad]
        out_shape.insert(0, jax.ShapeDtypeStruct((own_hidden, 4 * slots), jnp.bfloat16))
    out_specs = [pl.BlockSpec(o.shape, lambda i: (0, 0)) for o in out_shape]
    return pl.pallas_call(
        lambda *refs: gates_kernel(len(weights), *refs),
        grid=(1,),
        in_specs=in_specs,
        out_specs=out_specs,
        out_shape=out_shape,
        cost_estimate=pl.CostEstimate(
            flops=2 * high * width * slots,
            bytes_accessed=2 * (high * width + slots * width + 2 * high * slots),
            transcendentals=own_hidden * slots,
        ),
        compiler_params=pltpu.CompilerParams(vmem_limit_bytes=56 * MIB),
    )(*operands)


def part_kernel(shares, own_ref, *refs):
    weights, out_ref = refs[:shares], refs[-1]
    groups, _, low, _ = out_ref.shape
    depth = weights[0].shape[1]
    own = own_ref[...].T
    for d, weight in enumerate(weights):
        out_ref[:, 0, :, d * depth : (d + 1) * depth] = (
            jnp.dot(own, weight[...], preferred_element_type=jnp.float32)
            .astype(out_ref.dtype)
            .reshape(groups, low, depth)
        )


def slot_parts(own, weights, groups, lots, lot, earlier=None):
    high, slots = own.shape
    low = slots // groups
    width = weights[0].shape[1] * len(weights)
    more = [] if earlier is None else [earlier]
    return pl.pallas_call(
        lambda *refs: part_kernel(len(weights), *refs),
        grid=(1,),
        in_specs=[pl.BlockSpec((high, slots), lambda i: (0, 0))]
        + [pl.BlockSpec(weights[0].shape, lambda i: (0, 0))] * len(weights)
        + [pl.BlockSpec(memory_space=pl.ANY)] * len(more),
        out_specs=pl.BlockSpec((groups, 1, low, width), lambda i: (0, lot, 0, 0)),
        out_shape=jax.ShapeDtypeStruct((groups, lots, low, width), jnp.bfloat16),
        input_output_aliases={1 + len(weights): 0} if more else {},
        cost_estimate=pl.CostEstimate(
            flops=2 * high * width * slots,
            bytes_accessed=2 * (high * width + slots * width + high * slots),
            transcendentals=0,
        ),
        compiler_params=pltpu.CompilerParams(vmem_limit_bytes=56 * MIB),
    )(own, *weights, *more)


def combine_kernel(behind_ref, *refs):
    out_ref, half_refs = refs[-1], refs[:-1]
    sides, shares, half, features = out_ref.shape
    for q in range(shares):
        at = pl.ds(pl.multiple_of(behind_ref[q] * features, BLOCK), features)
        rows = jnp.zeros((sides * half, features), jnp.float32)
        for placing_ref, parts_ref in zip(half_refs[::2], half_refs[1::2]):
            rows = rows + jnp.dot(
                placing_ref[...], parts_ref[:, at], preferred_element_type=jnp.float32
            )
        rows = rows.astype(out_ref.dtype)
        for j in range(sides):
            out_ref[j, q] = rows[j * half : (j + 1) * half]


def combine(pairs, behind, sides):
    tok_rows = pairs[0][0].shape[0]
    width = pairs[0][1].shape[1]
    slots = sum(placing.shape[1] for placing, _ in pairs)
    shares = behind.shape[0]
    return pl.pallas_call(
        combine_kernel,
        in_specs=[pl.BlockSpec(memory_space=pltpu.SMEM)]
        + [pl.BlockSpec(memory_space=pltpu.VMEM)] * (2 * len(pairs)),
        out_specs=pl.BlockSpec(memory_space=pltpu.VMEM),
        out_shape=jax.ShapeDtypeStruct(
            (sides, shares, tok_rows // sides, width // shares), jnp.bfloat16
        ),
        cost_estimate=pl.CostEstimate(
            flops=2 * slots * tok_rows * width,
            bytes_accessed=2 * (slots * width + slots * tok_rows + tok_rows * width),
            transcendentals=0,
        ),
        compiler_params=pltpu.CompilerParams(vmem_limit_bytes=32 * MIB),
    )(behind, *[array for pair in pairs for array in pair])


def body(
    tokens,
    cotangent,
    gate_values,
    expert_ids,
    gate_weight,
    up_weight,
    down_weight,
    block_ids,
    feedback,
):
    groups = lax.axis_size("expert")
    shares = lax.axis_size("replica")
    sides = lax.axis_size("tensor")
    here = lax.axis_index("replica")
    experts = groups * gate_weight.shape[0]
    tok_rows, top_count = expert_ids.shape
    capacity = min(tok_rows, tok_rows * top_count * 3 // (2 * experts))
    features = tokens.shape[1]
    width = features * shares
    hidden = gate_weight.shape[2]
    own_hidden = hidden // shares
    stored = feedback[0]

    local_blocks = features // BLOCK
    local_ids = block_ids[0] - here * local_blocks
    holding = jnp.logical_and(local_ids >= 0, local_ids < local_blocks)
    held_at = jnp.clip(local_ids, 0, local_blocks - 1) * BLOCK
    select = local_ids.shape[0]

    pieces = split_weights(gate_weight[0], up_weight[0], here, shares)
    expert_ids, *pieces = lax.optimization_barrier((expert_ids, *pieces))

    def hand_out(d):
        return lax.ppermute(pieces[d], "replica", shift_by(d, shares))

    got = {d: hand_out(d) if d else pieces[0] for d in (0, 4, 3, 5, 2, 6, 1, 7)}

    padded = jnp.pad(tokens, ((0, SPARE), (0, 0)))
    gathered = lax.all_gather(padded, "replica", axis=0, tiled=False)

    low = capacity // 3
    lots = ((0, 1), (1, 1), (2, 1))
    lot_slots = [groups * count * low for _, count in lots]

    def lot_of(rows, lot):
        first, count = lots[lot]
        return rows[:, first * low : (first + count) * low].reshape(lot_slots[lot], -1)

    placing, slot_gate = routing_tables(expert_ids, gate_values, experts, capacity)
    sent_grads = (
        jnp.dot(placing, cotangent, preferred_element_type=jnp.float32) * slot_gate[:, None]
    ).astype(jnp.bfloat16)
    sent_grads = sent_grads.reshape(experts, capacity, features)
    stored_rows = pick_stored(stored, held_at, holding, lot_slots[2])
    sent_grads, stored_rows = lax.optimization_barrier((sent_grads, stored_rows))
    arrived_grads = lax.all_to_all(sent_grads, "expert", split_axis=0, concat_axis=0, tiled=True)
    w_down = down_weight[0]
    early = jnp.concatenate([lot_of(arrived_grads, 0), lot_of(arrived_grads, 1)], axis=0)
    hidden_first = hidden_product(w_down, early, None, shares)
    hidden_first, got[4] = lax.optimization_barrier((hidden_first, got[4]))
    hidden_second = hidden_product(w_down, lot_of(arrived_grads, 2), stored_rows, shares)
    grads_first = lax.psum_scatter(hidden_first, "replica", scatter_dimension=0, tiled=True)

    behind = (here - jnp.arange(shares, dtype=jnp.int32)) % shares
    whole_tokens = jnp.take(gathered[:, :tok_rows], behind, axis=0)
    whole_tokens = whole_tokens.transpose(1, 0, 2).reshape(tok_rows, width)
    sent_rows = jnp.dot(placing, whole_tokens, preferred_element_type=jnp.float32)
    sent_rows = sent_rows.astype(jnp.bfloat16).reshape(experts, capacity, width)
    sent_rows, hidden_second, got[1], got[7] = lax.optimization_barrier(
        (sent_rows, hidden_second, got[1], got[7])
    )
    arrived = lax.all_to_all(sent_rows, "expert", split_axis=0, concat_axis=0, tiled=True)
    hidden_second, arrived, *weights = lax.optimization_barrier(
        (hidden_second, arrived, *[got[d] for d in range(shares)])
    )
    grads_second = lax.psum_scatter(hidden_second, "replica", scatter_dimension=0, tiled=True)

    def give_back(parts):
        parts = parts.reshape(experts, -1, width)
        back = lax.all_to_all(parts, "expert", split_axis=0, concat_axis=0, tiled=True)
        return back.reshape(-1, width)

    tiles = arrived.reshape(groups, capacity // low, low, width)
    tile = lot_slots[0]
    (first,) = hidden_gates(weights, tiles, 0, grads_first, 0)
    back_first = give_back(slot_parts(first, weights, groups, 1, 0))
    (second,) = hidden_gates(weights, tiles, 1, grads_first, 1)
    parts = slot_parts(second, weights, groups, 2, 0)
    grads_second, second, parts, back_first = lax.optimization_barrier(
        (grads_second, second, parts, back_first)
    )
    shown, third = hidden_gates(weights, tiles, 2, grads_second, 0, (first, second))
    back_later = give_back(slot_parts(third, weights, groups, 2, 1, parts))

    shown = lax.all_gather(shown, "replica", axis=0, tiled=True)
    slots = sum(lot_slots)
    placed = (here - block_ids[0] // local_blocks) % shares
    picked_at = placed * features + block_ids[0] % local_blocks * BLOCK
    wanted = jnp.concatenate(
        [
            lax.dynamic_slice_in_dim(arrived, picked_at[i], BLOCK, axis=2)
            for i in range(select)
        ]
        + [arrived[:, :, :features]],
        axis=2,
    )
    wanted = jnp.concatenate([lot_of(wanted, lot) for lot in range(3)], axis=0)
    wanted = jnp.pad(wanted, ((0, shown.shape[1] - slots), (0, 0)))
    wanted, shown = lax.optimization_barrier((wanted, shown))
    products = jnp.einsum("sd,fs->df", wanted, shown, preferred_element_type=jnp.float32)
    block_sums = add_stored(products, shown, slots // tile, select)
    gradient = products[select * BLOCK :] + stored.astype(jnp.float32)
    struck = jnp.any(
        local_ids[:, None] == jnp.arange(local_blocks, dtype=jnp.int32)[None, :], axis=0
    )
    retained = (
        jnp.where(
            struck[:, None, None],
            jnp.float32(0.0),
            gradient.reshape(local_blocks, BLOCK, hidden),
        )
        .reshape(gradient.shape)
        .astype(jnp.bfloat16)
    )

    placing = placing.reshape(experts, capacity, tok_rows)
    placing_first = placing[:, :low].reshape(-1, tok_rows).T
    placing_later = placing[:, low:].reshape(-1, tok_rows).T
    combined = combine(
        [(placing_first, back_first), (placing_later, back_later)], behind, sides
    )
    combined = combined.reshape(sides * shares, tok_rows // sides, features)
    collected = lax.all_to_all(
        combined, ("tensor", "replica"), split_axis=0, concat_axis=0, tiled=True
    )
    collected, retained, block_sums = lax.optimization_barrier((collected, retained, block_sums))
    token_grad = jnp.sum(collected.astype(jnp.float32), axis=0).astype(jnp.bfloat16)
    return (token_grad, block_sums[None], retained[None])


def solution(mesh):
    return jax.shard_map(
        body,
        mesh=mesh,
        in_specs=(
            P("expert", "replica"),
            P("expert", "replica"),
            P("expert", None),
            P("expert", None),
            P("expert", "replica", "tensor"),
            P("expert", "replica", "tensor"),
            P("expert", "tensor", "replica"),
            P("expert", None),
            P("expert", "replica", "tensor"),
        ),
        out_specs=(
            P(("expert", "tensor"), "replica"),
            P("expert", None, None, "tensor"),
            P("expert", "replica", "tensor"),
        ),
        check_vma=False,
    )
```
